256 devices in a mesh: frame: 16 (over z_lo, y), token: 8 (over x, core), dp: 2 (over z_hi).
Axes of the slice: x: 4, y: 4, z: 8 (z_hi: 2, z_lo: 4; z = z_hi * 4 + z_lo), core: 2. Of those that a mesh axis runs over, the one named last changes fastest.
Arguments:
- temporal_qkv: bfloat16 [3, 2, 128, 128, 1024], P(None, 'dp', 'frame', 'token'), may hold values from -6 to 6
- spatial_qkv: bfloat16 [3, 2, 128, 128, 1024], P(None, 'dp', 'frame', 'token'), may hold values from -6 to 6
- out_grad: bfloat16 [2, 128, 128, 1024], P('dp', 'frame', 'token'), may hold values from -6 to 6
- temporal_proj: bfloat16 [1024, 1024], replicated, may hold values from -0.1875 to 0.1875
- spatial_proj: bfloat16 [1024, 1024], replicated, may hold values from -0.1875 to 0.1875
Outputs:
- temporal_qkv_grad: bfloat16 [3, 2, 128, 128, 1024], P(None, 'dp', 'frame', 'token')
- spatial_qkv_grad: bfloat16 [3, 2, 128, 128, 1024], P(None, 'dp', 'frame', 'token')
- temporal_proj_grad: float32 [1024, 1024], P('frame', ('token', 'dp'))
- spatial_proj_grad: float32 [1024, 1024], P('frame', ('token', 'dp'))
The draws below stay inside these ranges and needn't reach their ends.
All inputs are finite; a program needn't handle non-finite values.
Results may differ from the reference program's by a relative error of at most 0.025.
Values may be sent and summed in bfloat16 or wider, within the bound.
A program may use at most 128 MiB of HBM per device.

```python
import jax
import jax.numpy as jnp
from jax import lax

HEADS = 16
HEAD_DIM = 64
D = 1024
CLIPS = 2
FRAMES = 128
TOKENS = 128


def drawn_qkv(key):
    key_base = jax.random.fold_in(key, 0)
    full_shape = (3, CLIPS, FRAMES, TOKENS, D)
    return jnp.clip(jax.random.normal(key_base, full_shape, jnp.float32), -4.0, 4.0).astype(jnp.bfloat16)


def draw_temporal_qkv(key, part):
    return drawn_qkv(jax.random.fold_in(key, 11))


def draw_spatial_qkv(key, part):
    return drawn_qkv(jax.random.fold_in(key, 23))


def raised(drawn, own_key, source, target, parts, factor):
    def block_of(dim):
        return (jnp.arange(drawn.shape[dim]) // (drawn.shape[dim] // parts)).reshape((-1,) + (1,) * (drawn.ndim - 1 - dim))

    one_side = jax.random.permutation(own_key, parts)[block_of(target)]
    second = (block_of(target) + parts // 2) % parts
    return jnp.where((block_of(source) == one_side) | (block_of(source) == second), factor * drawn, drawn)


def level_of(rng, extent, cuts, least, largest):
    gain, own = 1.0, jax.random.fold_in(rng, 6)
    for axis_at, parts in cuts:
        draws = jnp.exp(jax.random.uniform(jax.random.fold_in(own, axis_at), (parts,), jnp.float32, least / len(cuts), largest / len(cuts)))
        gain = gain * jnp.repeat(draws, extent[axis_at] // parts).reshape([-1 if axis == axis_at else 1 for axis in range(len(extent))])
    return gain


def centred(own_key, shape, deviation, reach, shards=(), kind=jnp.bfloat16):
    result = jax.random.normal(own_key, shape, jnp.float32) * deviation
    if len(shards) > 0:
        result = level_of(own_key, shape, shards, -0.22, 0.18) * result
    return jnp.clip(result, min=-reach, max=reach).astype(kind)


def bell_draw_with(stream_key, shape, width, most, cuts, heavy, held_as=jnp.bfloat16):
    entries = width * jax.random.normal(stream_key, shape, jnp.float32)
    if cuts:
        entries = entries * level_of(stream_key, shape, cuts, -0.22, 0.18)
    return jnp.clip(raised(entries, jax.random.fold_in(stream_key, 3), *heavy), -most, most).astype(held_as)


def setup_inputs(seed: int = 0) -> dict:
    key_of = jax.random.split(jax.random.key(seed), 6)
    return {
        "temporal_qkv": draw_temporal_qkv(jax.random.fold_in(key_of[5], 71), 0),
        "spatial_qkv": draw_spatial_qkv(jax.random.fold_in(key_of[5], 71), 0),
        "out_grad": bell_draw_with(key_of[2], (CLIPS, FRAMES, TOKENS, D), 1.0, 6.0, ((0, 2), (1, 16), (2, 8)), (1, 3, 16, 2.0)),
        "temporal_proj": centred(key_of[3], (D, D), D ** -0.5, 0.1875),
        "spatial_proj": centred(key_of[4], (D, D), D ** -0.5, 0.1875),
    }


def split_heads(array_in, temporal):
    shaped = array_in.reshape(CLIPS, FRAMES, TOKENS, HEADS, HEAD_DIM)
    if temporal:
        return jnp.transpose(shaped, (3, 0, 2, 1, 4))
    return jnp.transpose(shaped, (3, 0, 1, 2, 4))


def merge_heads(array_in, temporal):
    if temporal:
        moved = jnp.transpose(array_in, (1, 3, 2, 0, 4))
    else:
        moved = jnp.transpose(array_in, (1, 2, 3, 0, 4))
    return moved.reshape(CLIPS, FRAMES, TOKENS, D)


def head_backward(pieces):
    query_h, key_h, value_h, upstream = pieces
    inv_root = HEAD_DIM ** -0.5
    query_f = query_h.astype(jnp.float32)
    key_f = key_h.astype(jnp.float32)
    value_f = value_h.astype(jnp.float32)
    upstream_f = upstream.astype(jnp.float32)
    scores = jnp.einsum("abie,abje->abij", query_f, key_f) * inv_root
    attn_probs = jax.nn.softmax(scores, axis=-1)
    probs_low = attn_probs.astype(jnp.bfloat16)
    attn_out = jnp.einsum("abij,abje->abie", probs_low.astype(jnp.float32), value_f).astype(jnp.bfloat16)
    prob_grad = jnp.einsum("abie,abje->abij", upstream_f, value_f)
    row_delta = jnp.sum(upstream_f * attn_out.astype(jnp.float32), axis=-1, keepdims=True)
    score_grad = (attn_probs * (prob_grad - row_delta)).astype(jnp.bfloat16).astype(jnp.float32)
    query_grad = (jnp.einsum("abij,abje->abie", score_grad, key_f) * inv_root).astype(jnp.bfloat16)
    key_grad = (jnp.einsum("abij,abie->abje", score_grad, query_f) * inv_root).astype(jnp.bfloat16)
    value_grad = jnp.einsum("abij,abie->abje", probs_low.astype(jnp.float32), upstream_f).astype(jnp.bfloat16)
    return attn_out, query_grad, key_grad, value_grad


def branch_grads(qkv_in, out_grad, projection, temporal):
    flat_grad = out_grad.reshape(-1, D)
    branch = jnp.dot(flat_grad, projection, preferred_element_type=jnp.float32).astype(jnp.bfloat16)
    branch = branch.reshape(out_grad.shape)
    head_split = tuple(split_heads(array_in, temporal) for array_in in (qkv_in[0], qkv_in[1], qkv_in[2], branch))
    attn_out, query_grad, key_grad, value_grad = lax.map(head_backward, head_split)
    merged_out = merge_heads(attn_out, temporal)
    all_grads = jnp.stack([merge_heads(one_grad, temporal) for one_grad in (query_grad, key_grad, value_grad)])
    proj_grad = jnp.dot(flat_grad.T, merged_out.reshape(-1, D), preferred_element_type=jnp.float32)
    return all_grads, proj_grad


def reference(temporal_qkv, spatial_qkv, out_grad, temporal_proj, spatial_proj):
    temporal_grads, temporal_proj_grad = branch_grads(temporal_qkv, out_grad, temporal_proj, True)
    spatial_grads, spatial_proj_grad = branch_grads(spatial_qkv, out_grad, spatial_proj, False)
    return temporal_grads, spatial_grads, temporal_proj_grad, spatial_proj_grad
```

```python
import jax
import jax.numpy as jnp
from jax import lax
from jax.sharding import PartitionSpec as P

HEADS = 16


def project(cotangent, projection):
    flat_rows = cotangent.reshape(-1, cotangent.shape[-1])
    result = jnp.dot(flat_rows, projection, preferred_element_type=jnp.float32)
    return result.astype(jnp.bfloat16).reshape(cotangent.shape)


def attend(qkv_block, branch_grad, temporal):
    grid_shape = branch_grad.shape
    head_shape = grid_shape[:3] + (HEADS, grid_shape[3] // HEADS)
    inv_root = (grid_shape[3] // HEADS) ** (-0.5)
    query_h = qkv_block[0].reshape(head_shape)
    key_h = qkv_block[1].reshape(head_shape)
    value_h = qkv_block[2].reshape(head_shape)
    upstream = branch_grad.reshape(head_shape)
    row_spec = "cibhe" if temporal else "cbihe"
    col_spec = "cjbhe" if temporal else "cbjhe"
    pair_spec = "cbhij"
    scores = (
        jnp.einsum(
            row_spec + "," + col_spec + "->" + pair_spec,
            query_h,
            key_h,
            preferred_element_type=jnp.float32,
        )
        * inv_root
    )
    attn_probs = jax.nn.softmax(scores, axis=-1)
    probs_low = attn_probs.astype(jnp.bfloat16)
    attn_out = jnp.einsum(
        pair_spec + "," + col_spec + "->" + row_spec,
        probs_low,
        value_h,
        preferred_element_type=jnp.float32,
    ).astype(jnp.bfloat16)
    prob_grad = jnp.einsum(
        row_spec + "," + col_spec + "->" + pair_spec,
        upstream,
        value_h,
        preferred_element_type=jnp.float32,
    )
    row_delta = jnp.einsum(
        row_spec + "," + row_spec + "->cbhi", upstream, attn_out, preferred_element_type=jnp.float32
    )
    score_grad = (attn_probs * (prob_grad - row_delta[..., None])).astype(jnp.bfloat16)
    query_grad = (
        jnp.einsum(
            pair_spec + "," + col_spec + "->" + row_spec,
            score_grad,
            key_h,
            preferred_element_type=jnp.float32,
        )
        * inv_root
    ).astype(jnp.bfloat16)
    key_grad = (
        jnp.einsum(
            pair_spec + "," + row_spec + "->" + col_spec,
            score_grad,
            query_h,
            preferred_element_type=jnp.float32,
        )
        * inv_root
    ).astype(jnp.bfloat16)
    value_grad = jnp.einsum(
        pair_spec + "," + row_spec + "->" + col_spec,
        probs_low,
        upstream,
        preferred_element_type=jnp.float32,
    ).astype(jnp.bfloat16)
    stacked = jnp.stack([query_grad, key_grad, value_grad]).reshape((3,) + grid_shape)
    return (attn_out.reshape(grid_shape), stacked)


def reduce_blocks(blocks, axis, dim):
    parts = lax.axis_size(axis)
    shape = blocks.shape
    cut = blocks.reshape(shape[:dim] + (parts, shape[dim] // parts) + shape[dim + 1 :])
    cut = jnp.moveaxis(cut, dim, 0)
    landed = lax.all_to_all(cut.astype(jnp.bfloat16), axis, split_axis=0, concat_axis=0, tiled=True)
    return jnp.sum(landed.astype(jnp.float32), axis=0)


def outer(cotangent, branch_out):
    width = cotangent.shape[-1]
    return jnp.einsum(
        "rd,re->de",
        cotangent.reshape(-1, width),
        branch_out.reshape(-1, width),
        preferred_element_type=jnp.float32,
    )


def local(temporal_qkv, spatial_qkv, out_grad, temporal_proj, spatial_proj):
    temporal_send = jnp.concatenate([temporal_qkv, out_grad[None]], axis=0)
    spatial_send = jnp.concatenate([spatial_qkv, out_grad[None]], axis=0)
    temporal_recv = lax.all_to_all(temporal_send, "frame", split_axis=3, concat_axis=2, tiled=True)
    spatial_recv = lax.all_to_all(spatial_send, "token", split_axis=2, concat_axis=3, tiled=True)
    temporal_branch = project(temporal_recv[3], temporal_proj)
    spatial_branch = project(spatial_recv[3], spatial_proj)
    temporal_out, temporal_grads = attend(temporal_recv[:3], temporal_branch, True)
    spatial_out, spatial_grads = attend(spatial_recv[:3], spatial_branch, False)
    temporal_home = lax.all_to_all(temporal_grads, "frame", split_axis=2, concat_axis=3, tiled=True)
    spatial_home = lax.all_to_all(spatial_grads, "token", split_axis=3, concat_axis=2, tiled=True)
    blocks = jnp.stack([outer(temporal_recv[3], temporal_out), outer(spatial_recv[3], spatial_out)])
    blocks = reduce_blocks(blocks, "token", 2)
    blocks = reduce_blocks(blocks, "frame", 1)
    blocks = reduce_blocks(blocks, "dp", 2)
    return (temporal_home, spatial_home, blocks[0], blocks[1])


def solution(mesh):
    in_specs = (
        P(None, "dp", "frame", "token", None),
        P(None, "dp", "frame", "token", None),
        P("dp", "frame", "token", None),
        P(),
        P(),
    )
    out_specs = (
        P(None, "dp", "frame", "token", None),
        P(None, "dp", "frame", "token", None),
        P("frame", ("token", "dp")),
        P("frame", ("token", "dp")),
    )
    return jax.shard_map(local, mesh=mesh, in_specs=in_specs, out_specs=out_specs, check_vma=False)
```

```python
import jax
import jax.numpy as jnp
from jax import lax
from jax.experimental import pallas as pl
from jax.experimental.pallas import tpu as pltpu
from jax.sharding import PartitionSpec as P

MESH = pl.DeviceIdType.MESH
BF16 = jnp.bfloat16
F32 = jnp.float32
ROOT = 0.125
CHUNKS = 2
PAIRS = 4


def rows_dot(left, right):
    return lax.dot_general(left, right, (((0,), (0,)), ((), ())), preferred_element_type=F32)


def cols_dot(left, right):
    return lax.dot_general(left, right, (((1,), (1,)), ((), ())), preferred_element_type=F32)


def dot(left, right):
    return jnp.dot(left, right, preferred_element_type=F32)


def attend_pair(q, k, v, g):
    lane = lax.broadcasted_iota(jnp.int32, (128, 128), 1)
    low = lane < 64
    low_b = low.astype(F32).astype(BF16)
    high_b = (lane >= 64).astype(F32).astype(BF16)
    q2 = jnp.concatenate([q * low_b, q * high_b], axis=0)
    g2 = jnp.concatenate([g * low_b, g * high_b], axis=0)
    scores = cols_dot(q2, k)
    top = jnp.max(scores, axis=1, keepdims=True)
    grown = jnp.exp((scores - top) * ROOT)
    probs = grown * (1.0 / jnp.sum(grown, axis=1, keepdims=True))
    probs_low = probs.astype(BF16)
    out2 = dot(probs_low, v)
    out = jnp.where(low, out2[:128], out2[128:]).astype(BF16)
    prob_grad = cols_dot(g2, v)
    out_f = out.astype(F32)
    delta = jnp.sum(g2.astype(F32) * jnp.concatenate([out_f, out_f], axis=0), axis=1, keepdims=True)
    score_grad = (probs * (prob_grad - delta)).astype(BF16)
    dq2 = dot(score_grad, k)
    dq = jnp.where(low, dq2[:128], dq2[128:]) * ROOT
    dk = rows_dot(score_grad, q2) * ROOT
    dv = rows_dot(probs_low, g2)
    return out, dq, dk, dv


def shuffle_matrix():
    row = lax.broadcasted_iota(jnp.int32, (128, 128), 0)
    col = lax.broadcasted_iota(jnp.int32, (128, 128), 1)
    hit = ((row >> 3) == (col & 15)) & ((row & 7) == (col >> 4))
    return hit.astype(F32).astype(BF16)


def body(
    tqkv_hbm, squkv_hbm, grad_hbm, tproj_hbm, sproj_hbm,
    tout_hbm, sout_hbm, tproj_out, sproj_out,
    tqkv, grad, tproj, sproj,
    tg_send, tg_recv, tc_send, tc_recv, tg, tbranch, tchunk, tgrad, tb_send, tb_recv, tout, tattn,
    sg, sq, sbranch, sgrad, sattn,
    tg_peer, tattn_peer, sg_peer, sattn_peer,
    tpart, tx_a, tx_b, tx_c, tx_sum, ty_send, ty_recv, tz_send, tz_recv,
    spart, sy_a, sy_b, sy_c, sy_sum, sx_send, sx_recv, sz_send, sz_recv,
    load_sem, tg_ss, tg_rs, tc_ss, tc_rs, tb_ss, tb_rs,
    sg_ss, sg_rs, sq_ss, sq_rs, sb_ss, sb_rs, own_sem,
    pg_ss, pg_rs, po_ss, po_rs, ring_ss, ring_rs, y_ss, y_rs, x_ss, x_rs, tz_ss, tz_rs, sz_ss, sz_rs, out_sem,
):
    frame = lax.axis_index("frame")
    token = lax.axis_index("token")
    dp = lax.axis_index("dp")
    z, y = frame // 4, lax.rem(frame, 4)
    x, core = token // 2, lax.rem(token, 2)
    zslot = dp * 4 + z

    def frame_peer(d):
        return lax.rem(frame + d, 16)

    def token_peer(d):
        return lax.rem(token + d, 8)

    def x_peer(d):
        return lax.rem(x + d, 4) * 2 + core

    def y_peer(d):
        return z * 4 + lax.rem(y + d, 4)

    def z_peer(d):
        slot = lax.rem(zslot + d, 8)
        return slot // 4, lax.rem(slot, 4)

    def remote(src, dst, send_sem, recv_sem, device):
        return pltpu.make_async_remote_copy(
            src_ref=src, dst_ref=dst, send_sem=send_sem, recv_sem=recv_sem, device_id=device, device_id_type=MESH
        )

    loads = [
        pltpu.make_async_copy(grad_hbm, grad, load_sem.at[0]),
        pltpu.make_async_copy(tqkv_hbm, tqkv, load_sem.at[1]),
        pltpu.make_async_copy(tproj_hbm, tproj, load_sem.at[2]),
        pltpu.make_async_copy(sproj_hbm, sproj, load_sem.at[3]),
    ]
    for load in loads:
        load.start()

    barrier = pltpu.get_barrier_semaphore()

    def greet_frame(d, carry):
        pl.semaphore_signal(barrier, inc=1, device_id={"frame": frame_peer(d)}, device_id_type=MESH)
        return carry

    def greet_token(d, carry):
        pl.semaphore_signal(barrier, inc=1, device_id={"token": token_peer(d)}, device_id_type=MESH)
        return carry

    def greet_dp(d, carry):
        pl.semaphore_signal(
            barrier, inc=1, device_id={"dp": 1 - dp, "frame": lax.rem(z + d, 4) * 4 + y}, device_id_type=MESH
        )
        return carry

    lax.fori_loop(1, 16, greet_frame, 0)
    lax.fori_loop(1, 8, greet_token, 0)
    lax.fori_loop(0, 4, greet_dp, 0)

    shuffle = shuffle_matrix()
    loads[0].wait()
    halves = []
    for half in range(2):
        rows = dot(shuffle, grad[:, :, half * 512 : half * 512 + 512].reshape(128, 512))
        halves.append(rows.reshape(16, 8, 512))
    tg_send[...] = jnp.concatenate(halves, axis=1).astype(BF16)

    pl.semaphore_wait(barrier, 26)

    def tg_copy(d):
        peer = frame_peer(d)
        return remote(tg_send.at[peer], tg_recv.at[frame], tg_ss.at[d], tg_rs.at[d], {"frame": peer})

    def tc_copy(chunk, d):
        peer = frame_peer(d)
        return remote(
            tc_send.at[chunk, peer], tc_recv.at[chunk, frame], tc_ss.at[chunk, d], tc_rs.at[chunk, d], {"frame": peer}
        )

    def tb_copy(chunk, d):
        peer = frame_peer(d)
        return remote(
            tb_send.at[chunk, peer], tb_recv.at[chunk, frame], tb_ss.at[chunk, d], tb_rs.at[chunk, d], {"frame": peer}
        )

    def token_rows(who):
        return pl.ds(pl.multiple_of(who * 16, 16), 16)

    def sg_copy(d):
        peer = token_peer(d)
        return remote(grad_hbm.at[peer], sg.at[token_rows(token)], sg_ss.at[d], sg_rs.at[d], {"token": peer})

    def sq_copy(d):
        peer = token_peer(d)
        return remote(squkv_hbm.at[:, peer], sq.at[:, token_rows(token)], sq_ss.at[d], sq_rs.at[d], {"token": peer})

    def sb_copy(d):
        peer = token_peer(d)
        return remote(sgrad.at[:, token_rows(peer)], sout_hbm.at[:, token], sb_ss.at[d], sb_rs.at[d], {"token": peer})

    def each(low, high, make, act):
        def step(d, carry):
            act(make(d))
            return carry

        lax.fori_loop(low, high, step, 0)

    def start(copy):
        copy.start()

    def arrive(copy):
        copy.wait_recv()

    def leave(copy):
        copy.wait_send()

    each(1, 16, tg_copy, start)
    each(1, 8, sg_copy, start)
    own_g = pltpu.make_async_copy(grad_hbm.at[token], sg.at[token_rows(token)], own_sem.at[0])
    own_q = pltpu.make_async_copy(squkv_hbm.at[:, token], sq.at[:, token_rows(token)], own_sem.at[1])
    own_g.start()
    own_q.start()
    each(1, 8, sq_copy, start)

    loads[1].wait()
    for chunk in range(CHUNKS):
        for a in range(3):
            pieces = []
            for i in range(PAIRS):
                at = (2 * i + chunk) * 128
                rows = dot(shuffle, tqkv[a, :, :, at : at + 128].reshape(128, 128))
                pieces.append(rows.reshape(16, 8, 128))
            first = jnp.concatenate(pieces[:2], axis=2)
            second = jnp.concatenate(pieces[2:], axis=2)
            tc_send[chunk, :, a * 16 : a * 16 + 16, :] = jnp.concatenate([first, second], axis=1).astype(BF16)
        each(1, 16, lambda d: tc_copy(chunk, d), start)
        tc_recv[chunk, frame] = tc_send[chunk, frame]
    tg_recv[frame] = tg_send[frame]

    peer_core = {"token": token + 1 - 2 * core}
    each(1, 16, tg_copy, arrive)
    loads[2].wait()
    landed = tg_recv[...].astype(F32).reshape(16, 2, 8, 512)
    for half in range(2):
        tg[:, half * 512 : half * 512 + 512] = landed[:, half].reshape(128, 512).astype(BF16)
    tg_pair = remote(tg, tg_peer, pg_ss.at[0], pg_rs.at[0], peer_core)
    tg_pair.start()
    for col in range(0, 1024, 256):
        tbranch[:, col : col + 256] = dot(tg[...], tproj[:, col : col + 256]).astype(BF16)

    own_g.wait()
    each(1, 8, sg_copy, arrive)
    loads[3].wait()
    sg_pair = remote(sg, sg_peer, pg_ss.at[1], pg_rs.at[1], peer_core)
    sg_pair.start()
    for col in range(0, 1024, 256):
        sbranch[:, col : col + 256] = dot(sg[...], sproj[:, col : col + 256]).astype(BF16)

    def temporal_chunk(chunk):
        each(1, 16, lambda d: tc_copy(chunk, d), arrive)
        for a in range(3):
            block = tc_recv[chunk, :, a * 16 : a * 16 + 16, :].astype(F32).reshape(16, 2, 8, 256)
            for half in range(2):
                tchunk[a, :, half * 256 : half * 256 + 256] = block[:, half].reshape(128, 256).astype(BF16)

        def pair(i, carry):
            here = pl.ds(pl.multiple_of(i * 128, 128), 128)
            there = pl.ds(pl.multiple_of((2 * i + chunk) * 128, 128), 128)
            out, dq, dk, dv = attend_pair(tchunk[0, :, here], tchunk[1, :, here], tchunk[2, :, here], tbranch[:, there])
            tattn[chunk, :, here] = out
            tgrad[0, :, here] = dq
            tgrad[1, :, here] = dk
            tgrad[2, :, here] = dv
            return carry

        lax.fori_loop(0, PAIRS, pair, 0)
        for a in range(3):
            rows = tgrad[a].reshape(16, 8, 512)
            tb_send[chunk, :, a * 16 : a * 16 + 16, :] = jnp.concatenate(
                [rows[:, :, :256], rows[:, :, 256:]], axis=1
            ).astype(BF16)
        each(1, 16, lambda d: tb_copy(chunk, d), start)
        tb_recv[chunk, frame] = tb_send[chunk, frame]

    tattn_pair = remote(tattn.at[1 - core], tattn_peer, po_ss.at[0], po_rs.at[0], peer_core)
    sattn_pair = remote(sattn.at[1 - core], sattn_peer, po_ss.at[1], po_rs.at[1], peer_core)

    left_x, right_x = {"token": x_peer(3)}, {"token": x_peer(1)}
    left_y, right_y = {"frame": y_peer(3)}, {"frame": y_peer(1)}
    tx_copies = [
        remote(tpart.at[lax.rem(x + 2, 4)], tx_a, ring_ss.at[0], ring_rs.at[0], left_x),
        remote(tpart.at[lax.rem(x + 1, 4)], tx_b, ring_ss.at[1], ring_rs.at[1], right_x),
        remote(tx_sum, tx_c, ring_ss.at[2], ring_rs.at[2], left_x),
    ]
    sy_copies = [
        remote(spart.at[lax.rem(y + 2, 4)], sy_a, ring_ss.at[3], ring_rs.at[3], left_y),
        remote(spart.at[lax.rem(y + 1, 4)], sy_b, ring_ss.at[4], ring_rs.at[4], right_y),
        remote(sy_sum, sy_c, ring_ss.at[5], ring_rs.at[5], left_y),
    ]

    def temporal_partial(chunk):
        tg_pair.wait_recv()
        tattn_pair.wait_recv()
        rows_g = jnp.concatenate([tg[...], tg_peer[...]], axis=0)
        rows_o = jnp.concatenate([tattn[chunk], tattn_peer[...]], axis=0)
        for block in range(4):
            part = rows_dot(rows_g[:, block * 256 : block * 256 + 256], rows_o).astype(BF16)
            for i in range(4):
                tpart[i, block * 256 : block * 256 + 256, :] = part[:, i * 128 : i * 128 + 128]
        tx_copies[0].start()
        tx_copies[1].start()

    def temporal_relay():
        tx_copies[0].wait_recv()
        tx_sum[...] = (tpart[lax.rem(x + 3, 4)].astype(F32) + tx_a[...].astype(F32)).astype(BF16)
        tx_copies[2].start()

    temporal_chunk(0)

    @pl.when(core == 1)
    def _():
        tattn_pair.start()

    @pl.when(core == 0)
    def _():
        temporal_partial(0)

    own_q.wait()
    each(1, 8, sq_copy, arrive)

    def spatial_pair(i, carry):
        for c in range(2):
            at = pl.ds(pl.multiple_of((2 * i + c) * 128, 128), 128)
            here = pl.ds(pl.multiple_of(i * 128, 128), 128)
            out, dq, dk, dv = attend_pair(sq[0, :, at], sq[1, :, at], sq[2, :, at], sbranch[:, at])
            sattn[c, :, here] = out
            sgrad[0, :, at] = dq.astype(BF16)
            sgrad[1, :, at] = dk.astype(BF16)
            sgrad[2, :, at] = dv.astype(BF16)
        return carry

    lax.fori_loop(0, 4, spatial_pair, 0)
    sattn_pair.start()
    each(1, 8, sb_copy, start)
    own_b = pltpu.make_async_copy(sgrad.at[:, token_rows(token)], sout_hbm.at[:, token], own_sem.at[2])
    own_b.start()

    @pl.when(core == 0)
    def _():
        temporal_relay()

    sg_pair.wait_recv()
    sattn_pair.wait_recv()
    rows_g = jnp.concatenate([sg[...], sg_peer[...]], axis=0)
    rows_o = jnp.concatenate([sattn[core], sattn_peer[...]], axis=0)
    for block in range(4):
        part = rows_dot(rows_g[:, block * 256 : block * 256 + 256], rows_o).astype(BF16)
        for i in range(4):
            spart[i, block * 64 : block * 64 + 64, :] = part[i * 64 : i * 64 + 64]
    sy_copies[0].start()
    sy_copies[1].start()

    temporal_chunk(1)

    @pl.when(core == 0)
    def _():
        tattn_pair.start()

    @pl.when(core == 1)
    def _():
        temporal_partial(1)

    sy_copies[0].wait_recv()
    sy_sum[...] = (spart[lax.rem(y + 3, 4)].astype(F32) + sy_a[...].astype(F32)).astype(BF16)
    sy_copies[2].start()

    @pl.when(core == 1)
    def _():
        temporal_relay()

    def sx_copy(d):
        to = lax.rem(x + d, 4)
        return remote(sx_send.at[to], sx_recv.at[x], x_ss.at[d], x_rs.at[d], {"token": to * 2 + core})

    def ty_copy(d):
        to = lax.rem(y + d, 4)
        return remote(ty_send.at[to], ty_recv.at[y], y_ss.at[d], y_rs.at[d], {"frame": z * 4 + to})

    def z_copy(send, recv, ss, rs, d):
        to_dp, to_z = z_peer(d)
        return remote(send.at[to_z], recv.at[zslot], ss.at[d], rs.at[d], {"dp": to_dp, "frame": to_z * 4 + y})

    def tz_copy(d):
        return z_copy(tz_send, tz_recv, tz_ss, tz_rs, d)

    def sz_copy(d):
        return z_copy(sz_send, sz_recv, sz_ss, sz_rs, d)

    sy_copies[1].wait_recv()
    sy_copies[2].wait_recv()
    total = spart[y].astype(F32) + sy_b[...].astype(F32) + sy_c[...].astype(F32)
    for i in range(4):
        sx_send[i] = total[:, i * 128 : i * 128 + 128].astype(BF16)
    each(1, 4, sx_copy, start)

    tx_copies[1].wait_recv()
    tx_copies[2].wait_recv()
    total = tpart[x].astype(F32) + tx_b[...].astype(F32) + tx_c[...].astype(F32)
    for block in range(4):
        for i in range(4):
            at = block * 256 + i * 64
            ty_send[i, block * 64 : block * 64 + 64, :] = total[at : at + 64].astype(BF16)
    each(1, 4, ty_copy, start)

    sx_recv[x] = sx_send[x]
    each(1, 4, sx_copy, arrive)
    total = jnp.sum(sx_recv[...].astype(F32), axis=0).reshape(4, 64, 128)
    sz_send[...] = total.astype(BF16)
    each(1, 8, sz_copy, start)
    sz_recv[zslot] = sz_send[z]

    ty_recv[y] = ty_send[y]
    each(1, 4, ty_copy, arrive)
    total = jnp.sum(ty_recv[...].astype(F32), axis=0).reshape(4, 64, 128)
    tz_send[...] = total.astype(BF16)
    each(1, 8, tz_copy, start)
    tz_recv[zslot] = tz_send[z]

    for chunk in range(CHUNKS):
        each(1, 16, lambda d: tb_copy(chunk, d), arrive)
        for a in range(3):
            block = tb_recv[chunk, :, a * 16 : a * 16 + 16, :].astype(F32).reshape(16, 2, 8, 256)
            for half in range(2):
                rows = rows_dot(shuffle, block[:, half].reshape(128, 256).astype(BF16)).astype(BF16)
                for i in range(2):
                    at = (2 * (2 * half + i) + chunk) * 128
                    tout[a, :, :, at : at + 128] = rows[:, i * 128 : i * 128 + 128].reshape(8, 16, 128)
    store = pltpu.make_async_copy(tout, tout_hbm, out_sem)
    store.start()

    each(1, 8, sz_copy, arrive)
    total = jnp.sum(sz_recv[...].astype(F32), axis=0)
    sproj_out[...] = jnp.where(dp == 1, total[:, 64:], total[:, :64])
    each(1, 8, tz_copy, arrive)
    total = jnp.sum(tz_recv[...].astype(F32), axis=0)
    tproj_out[...] = jnp.where(dp == 1, total[:, 64:], total[:, :64])

    each(1, 8, sb_copy, arrive)
    each(1, 16, tg_copy, leave)
    for chunk in range(CHUNKS):
        each(1, 16, lambda d: tc_copy(chunk, d), leave)
        each(1, 16, lambda d: tb_copy(chunk, d), leave)
    each(1, 8, sg_copy, leave)
    each(1, 8, sq_copy, leave)
    each(1, 8, sb_copy, leave)
    each(1, 4, sx_copy, leave)
    each(1, 4, ty_copy, leave)
    each(1, 8, sz_copy, leave)
    each(1, 8, tz_copy, leave)
    for copy in [tg_pair, sg_pair, tattn_pair, sattn_pair] + tx_copies + sy_copies:
        copy.wait_send()
    own_b.wait()
    store.wait()


def local(temporal_qkv, spatial_qkv, out_grad, temporal_proj, spatial_proj):
    def vm(*shape):
        return pltpu.VMEM(shape, BF16)

    def dma(*shape):
        return pltpu.SemaphoreType.DMA(shape)

    any_spec = pl.BlockSpec(memory_space=pl.ANY)
    vmem_spec = pl.BlockSpec(memory_space=pltpu.VMEM)
    tout, sout, tproj, sproj = pl.pallas_call(
        body,
        out_shape=(
            jax.ShapeDtypeStruct((3, 8, 16, 1024), BF16),
            jax.ShapeDtypeStruct((3, 8, 16, 1024), BF16),
            jax.ShapeDtypeStruct((64, 64), F32),
            jax.ShapeDtypeStruct((64, 64), F32),
        ),
        in_specs=[any_spec] * 5,
        out_specs=(any_spec, any_spec, vmem_spec, vmem_spec),
        scratch_shapes=[
            vm(3, 8, 16, 1024), vm(8, 16, 1024), vm(1024, 1024), vm(1024, 1024),
            vm(16, 16, 512), vm(16, 16, 512), vm(2, 16, 48, 256), vm(2, 16, 48, 256),
            vm(128, 1024), vm(128, 1024), vm(3, 128, 512), pltpu.VMEM((3, 128, 512), F32),
            vm(2, 16, 48, 256), vm(2, 16, 48, 256), vm(3, 8, 16, 1024), vm(2, 128, 512),
            vm(128, 1024), vm(3, 128, 1024), vm(128, 1024), vm(3, 128, 1024), vm(2, 128, 512),
            vm(128, 1024), vm(128, 512), vm(128, 1024), vm(128, 512),
            vm(4, 1024, 128), vm(1024, 128), vm(1024, 128), vm(1024, 128), vm(1024, 128),
            vm(4, 256, 128), vm(4, 256, 128), vm(4, 64, 128), vm(8, 64, 128),
            vm(4, 256, 512), vm(256, 512), vm(256, 512), vm(256, 512), vm(256, 512),
            vm(4, 256, 128), vm(4, 256, 128), vm(4, 64, 128), vm(8, 64, 128),
            dma(4), dma(16), dma(16), dma(2, 16), dma(2, 16), dma(2, 16), dma(2, 16),
            dma(8), dma(8), dma(8), dma(8), dma(8), dma(8), dma(3),
            dma(2), dma(2), dma(2), dma(2), dma(6), dma(6), dma(4), dma(4), dma(4), dma(4),
            dma(8), dma(8), dma(8), dma(8), pltpu.SemaphoreType.DMA,
        ],
        compiler_params=pltpu.CompilerParams(
            collective_id=0, has_side_effects=True, vmem_limit_bytes=48 * 1024 * 1024
        ),
    )(
        temporal_qkv.reshape(3, 8, 16, 1024),
        spatial_qkv.reshape(3, 8, 16, 1024),
        out_grad.reshape(8, 16, 1024),
        temporal_proj,
        spatial_proj,
    )
    shape = (3, 1, 8, 16, 1024)
    return tout.reshape(shape), sout.reshape(shape), tproj, sproj


def solution(mesh):
    in_specs = (
        P(None, "dp", "frame", "token", None),
        P(None, "dp", "frame", "token", None),
        P("dp", "frame", "token", None),
        P(),
        P(),
    )
    out_specs = (
        P(None, "dp", "frame", "token", None),
        P(None, "dp", "frame", "token", None),
        P("frame", ("token", "dp")),
        P("frame", ("token", "dp")),
    )
    return jax.shard_map(local, mesh=mesh, in_specs=in_specs, out_specs=out_specs, check_vma=False)
```

```python
import jax
import jax.numpy as jnp
from jax import lax
from jax.experimental import pallas as pl
from jax.experimental.pallas import tpu as pltpu
from jax.sharding import PartitionSpec as P

MESH = pl.DeviceIdType.MESH
BF16 = jnp.bfloat16
F32 = jnp.float32
ROOT = 0.125
CHUNKS = 2
PAIRS = 4


def rows_dot(left, right):
    return lax.dot_general(left, right, (((0,), (0,)), ((), ())), preferred_element_type=F32)


def cols_dot(left, right):
    return lax.dot_general(left, right, (((1,), (1,)), ((), ())), preferred_element_type=F32)


def dot(left, right):
    return jnp.dot(left, right, preferred_element_type=F32)


def attend_pair(q, k, v, g):
    lane = lax.broadcasted_iota(jnp.int32, (128, 128), 1)
    low = lane < 64
    low_b = low.astype(F32).astype(BF16)
    high_b = (lane >= 64).astype(F32).astype(BF16)
    q2 = jnp.concatenate([q * low_b, q * high_b], axis=0)
    g2 = jnp.concatenate([g * low_b, g * high_b], axis=0)
    scores = cols_dot(q2, k)
    top = jnp.max(scores, axis=1, keepdims=True)
    grown = jnp.exp((scores - top) * ROOT)
    probs = grown * (1.0 / jnp.sum(grown, axis=1, keepdims=True))
    probs_low = probs.astype(BF16)
    out2 = dot(probs_low, v)
    out = jnp.where(low, out2[:128], out2[128:]).astype(BF16)
    prob_grad = cols_dot(g2, v)
    out_f = out.astype(F32)
    delta = jnp.sum(g2.astype(F32) * jnp.concatenate([out_f, out_f], axis=0), axis=1, keepdims=True)
    score_grad = (probs * (prob_grad - delta)).astype(BF16)
    dq2 = dot(score_grad, k)
    dq = jnp.where(low, dq2[:128], dq2[128:]) * ROOT
    dk = rows_dot(score_grad, q2) * ROOT
    dv = rows_dot(probs_low, g2)
    return out, dq, dk, dv


def shuffle_matrix():
    row = lax.broadcasted_iota(jnp.int32, (128, 128), 0)
    col = lax.broadcasted_iota(jnp.int32, (128, 128), 1)
    hit = ((row >> 3) == (col & 15)) & ((row & 7) == (col >> 4))
    return hit.astype(F32).astype(BF16)


def body(
    tqkv_hbm, squkv_hbm, grad_hbm, tproj_hbm, sproj_hbm,
    tout_hbm, sout_hbm, tproj_out, sproj_out,
    tqkv, grad, tproj, sproj,
    tg_send, tg_recv, tc_send, tc_recv, tg_all, tbranch, tchunk, tgrad, tb_send, tb_recv, tout, tattn,
    sg, sq, sbranch, sgrad, sattn,
    tattn_all, sg_peer, sattn_peer,
    ty_send, ty_recv, tz_send, tz_recv,
    spart, sy_a, sy_b, sy_c, sy_sum, sx_send, sx_recv, sz_send, sz_recv,
    load_sem, tg_ss, tg_rs, tc_ss, tc_rs, tb_ss, tb_rs,
    sg_ss, sg_rs, sq_ss, sq_rs, sb_ss, sb_rs, own_sem,
    pair_ss, pair_rs, ta_ss, ta_rs, tf_ss, tf_rs, to_ss, to_rs, ring_ss, ring_rs, ty_ss, ty_rs, sx_ss, sx_rs, tz_ss, tz_rs, sz_ss, sz_rs, out_sem,
):
    frame = lax.axis_index("frame")
    token = lax.axis_index("token")
    dp = lax.axis_index("dp")
    z, y = frame // 4, lax.rem(frame, 4)
    x, core = token // 2, lax.rem(token, 2)
    zslot = dp * 4 + z

    def frame_peer(d):
        return lax.rem(frame + d, 16)

    def token_peer(d):
        return lax.rem(token + d, 8)

    def x_peer(d):
        return lax.rem(x + d, 4) * 2 + core

    def y_peer(d):
        return z * 4 + lax.rem(y + d, 4)

    def remote(src, dst, send_sem, recv_sem, device):
        return pltpu.make_async_remote_copy(
            src_ref=src, dst_ref=dst, send_sem=send_sem, recv_sem=recv_sem, device_id=device, device_id_type=MESH
        )

    loads = [
        pltpu.make_async_copy(grad_hbm, grad, load_sem.at[0]),
        pltpu.make_async_copy(tqkv_hbm, tqkv, load_sem.at[1]),
        pltpu.make_async_copy(tproj_hbm, tproj, load_sem.at[2]),
        pltpu.make_async_copy(sproj_hbm, sproj, load_sem.at[3]),
    ]
    for load in loads:
        load.start()

    barrier = pltpu.get_barrier_semaphore()

    def greet_frame(d, carry):
        pl.semaphore_signal(barrier, inc=1, device_id={"frame": frame_peer(d)}, device_id_type=MESH)
        return carry

    def greet_token(d, carry):
        pl.semaphore_signal(barrier, inc=1, device_id={"token": token_peer(d)}, device_id_type=MESH)
        return carry

    def greet_dp(d, carry):
        pl.semaphore_signal(
            barrier, inc=1, device_id={"dp": 1 - dp, "frame": lax.rem(z + d, 4) * 4 + y}, device_id_type=MESH
        )
        return carry

    lax.fori_loop(1, 16, greet_frame, 0)
    lax.fori_loop(1, 8, greet_token, 0)
    lax.fori_loop(0, 4, greet_dp, 0)

    shuffle = shuffle_matrix()
    loads[0].wait()
    halves = []
    for half in range(2):
        rows = dot(shuffle, grad[:, :, half * 512 : half * 512 + 512].reshape(128, 512))
        halves.append(rows.reshape(16, 8, 512))
    tg_send[...] = jnp.concatenate(halves, axis=1).astype(BF16)

    loads[1].wait()
    for chunk in range(CHUNKS):
        for a in range(3):
            pieces = []
            for i in range(PAIRS):
                at = (2 * i + chunk) * 128
                rows = dot(shuffle, tqkv[a, :, :, at : at + 128].reshape(128, 128))
                pieces.append(rows.reshape(16, 8, 128))
            first = jnp.concatenate(pieces[:2], axis=2)
            second = jnp.concatenate(pieces[2:], axis=2)
            tc_send[chunk, :, a * 16 : a * 16 + 16, :] = jnp.concatenate([first, second], axis=1).astype(BF16)
        tc_recv[chunk, frame] = tc_send[chunk, frame]
    tg_recv[frame] = tg_send[frame]

    pl.semaphore_wait(barrier, 26)

    def tg_copy(d):
        peer = frame_peer(d)
        return remote(tg_send.at[peer], tg_recv.at[frame], tg_ss.at[d], tg_rs.at[d], {"frame": peer})

    def tc_copy(chunk, d):
        peer = frame_peer(d)
        return remote(
            tc_send.at[chunk, peer], tc_recv.at[chunk, frame], tc_ss.at[chunk, d], tc_rs.at[chunk, d], {"frame": peer}
        )

    def tb_copy(chunk, d):
        peer = frame_peer(d)
        return remote(
            tb_send.at[chunk, peer], tb_recv.at[chunk, frame], tb_ss.at[chunk, d], tb_rs.at[chunk, d], {"frame": peer}
        )

    def token_rows(who):
        return pl.ds(pl.multiple_of(who * 16, 16), 16)

    def sg_copy(d):
        peer = token_peer(d)
        return remote(grad_hbm.at[peer], sg.at[token_rows(token)], sg_ss.at[d], sg_rs.at[d], {"token": peer})

    def sq_copy(d):
        peer = token_peer(d)
        return remote(squkv_hbm.at[:, peer], sq.at[:, token_rows(token)], sq_ss.at[d], sq_rs.at[d], {"token": peer})

    def sb_copy(d):
        peer = token_peer(d)
        return remote(sgrad.at[:, token_rows(peer)], sout_hbm.at[:, token], sb_ss.at[d], sb_rs.at[d], {"token": peer})

    def each(low, high, make, act):
        def step(d, carry):
            act(make(d))
            return carry

        lax.fori_loop(low, high, step, 0)

    def start(copy):
        copy.start()

    def arrive(copy):
        copy.wait_recv()

    def leave(copy):
        copy.wait_send()

    each(1, 16, tg_copy, start)
    each(1, 16, lambda d: tc_copy(0, d), start)
    each(1, 8, sg_copy, start)
    own_g = pltpu.make_async_copy(grad_hbm.at[token], sg.at[token_rows(token)], own_sem.at[0])
    own_q = pltpu.make_async_copy(squkv_hbm.at[:, token], sq.at[:, token_rows(token)], own_sem.at[1])
    own_g.start()
    own_q.start()
    each(1, 8, sq_copy, start)

    each(1, 16, lambda d: tc_copy(1, d), start)

    peer_core = {"token": token + 1 - 2 * core}
    each(1, 16, tg_copy, arrive)
    loads[2].wait()
    landed = tg_recv[...].astype(F32).reshape(16, 2, 8, 512)
    for half in range(2):
        tg_all[token, :, half * 512 : half * 512 + 512] = landed[:, half].reshape(128, 512).astype(BF16)

    def ta_copy(d):
        to = lax.rem(x + d, 4) * 2 + core
        return remote(tg_all.at[token], tg_all.at[token], ta_ss.at[d], ta_rs.at[d], {"token": to})

    def tf_copy(d):
        of = lax.rem(x + 4 - d, 4) * 2 + core
        return remote(tg_all.at[of], tg_all.at[of], tf_ss.at[d], tf_rs.at[d], peer_core)

    each(1, 4, ta_copy, start)
    tf_copy(0).start()
    for col in range(0, 1024, 256):
        tbranch[:, col : col + 256] = dot(tg_all[token], tproj[:, col : col + 256]).astype(BF16)

    own_g.wait()
    each(1, 8, sg_copy, arrive)
    loads[3].wait()
    sg_pair = remote(sg, sg_peer, pair_ss.at[0], pair_rs.at[0], peer_core)
    sg_pair.start()
    for col in range(0, 1024, 256):
        sbranch[:, col : col + 256] = dot(sg[...], sproj[:, col : col + 256]).astype(BF16)

    def to_copy(d):
        peer = token_peer(d)
        return remote(tattn.at[peer], tattn_all.at[token], to_ss.at[d], to_rs.at[d], {"token": peer})

    def temporal_chunk(chunk):
        each(1, 16, lambda d: tc_copy(chunk, d), arrive)
        for a in range(3):
            block = tc_recv[chunk, :, a * 16 : a * 16 + 16, :].astype(F32).reshape(16, 2, 8, 256)
            for half in range(2):
                tchunk[a, :, half * 256 : half * 256 + 256] = block[:, half].reshape(128, 256).astype(BF16)

        def pair(i, carry):
            here = pl.ds(pl.multiple_of(i * 128, 128), 128)
            there = pl.ds(pl.multiple_of((2 * i + chunk) * 128, 128), 128)
            out, dq, dk, dv = attend_pair(tchunk[0, :, here], tchunk[1, :, here], tchunk[2, :, here], tbranch[:, there])
            tattn[2 * i + chunk] = out
            tgrad[0, :, here] = dq
            tgrad[1, :, here] = dk
            tgrad[2, :, here] = dv
            return carry

        lax.fori_loop(0, PAIRS, pair, 0, unroll=True)
        if chunk == 1:
            each(1, 8, to_copy, start)
            tattn_all[token] = tattn[token]
        for a in range(3):
            rows = tgrad[a].reshape(16, 8, 512)
            tb_send[chunk, :, a * 16 : a * 16 + 16, :] = jnp.concatenate(
                [rows[:, :, :256], rows[:, :, 256:]], axis=1
            ).astype(BF16)
        each(1, 16, lambda d: tb_copy(chunk, d), start)
        tb_recv[chunk, frame] = tb_send[chunk, frame]

    sattn_pair = remote(sattn.at[1 - core], sattn_peer, pair_ss.at[1], pair_rs.at[1], peer_core)
    left, right = 3 - 2 * core, 1 + 2 * core
    left_y, right_y = {"frame": y_peer(left)}, {"frame": y_peer(right)}
    sy_copies = [
        remote(spart.at[lax.rem(y + 2, 4)], sy_a, ring_ss.at[0], ring_rs.at[0], left_y),
        remote(spart.at[lax.rem(y + right, 4)], sy_b, ring_ss.at[1], ring_rs.at[1], right_y),
        remote(sy_sum, sy_c, ring_ss.at[2], ring_rs.at[2], left_y),
    ]

    temporal_chunk(0)

    own_q.wait()
    each(1, 8, sq_copy, arrive)

    def spatial_pair(i, carry):
        for c in range(2):
            at = pl.ds(pl.multiple_of((2 * i + c) * 128, 128), 128)
            here = pl.ds(pl.multiple_of(i * 128, 128), 128)
            out, dq, dk, dv = attend_pair(sq[0, :, at], sq[1, :, at], sq[2, :, at], sbranch[:, at])
            sattn[c, :, here] = out
            sgrad[0, :, at] = dq.astype(BF16)
            sgrad[1, :, at] = dk.astype(BF16)
            sgrad[2, :, at] = dv.astype(BF16)
        return carry

    lax.fori_loop(0, 4, spatial_pair, 0, unroll=True)
    sattn_pair.start()
    each(1, 8, sb_copy, start)
    own_b = pltpu.make_async_copy(sgrad.at[:, token_rows(token)], sout_hbm.at[:, token], own_sem.at[2])
    own_b.start()

    sg_pair.wait_recv()
    sattn_pair.wait_recv()
    rows_g = jnp.concatenate([sg[...], sg_peer[...]], axis=0)
    rows_o = jnp.concatenate([sattn[core], sattn_peer[...]], axis=0)
    for block in range(4):
        part = rows_dot(rows_g[:, block * 256 : block * 256 + 256], rows_o).astype(BF16)
        for i in range(4):
            spart[i, block * 64 : block * 64 + 64, :] = part[i * 64 : i * 64 + 64]
    sy_copies[0].start()
    sy_copies[1].start()

    each(1, 4, ta_copy, arrive)
    each(1, 4, tf_copy, start)

    temporal_chunk(1)

    sy_copies[0].wait_recv()
    sy_sum[...] = (spart[lax.rem(y + left, 4)].astype(F32) + sy_a[...].astype(F32)).astype(BF16)
    sy_copies[2].start()


    def z_copy(send, recv, ss, rs, d):
        to = lax.rem(zslot + d, 8)
        return remote(send.at[to], recv.at[zslot], ss.at[d], rs.at[d], {"dp": to // 4, "frame": lax.rem(to, 4) * 4 + y})

    def ty_copy(d):
        to = lax.rem(y + d, 4)
        return remote(ty_send.at[to], ty_recv.at[y], ty_ss.at[d], ty_rs.at[d], {"frame": z * 4 + to})

    def sx_copy(d):
        to = lax.rem(x + d, 4)
        return remote(sx_send.at[to], sx_recv.at[x], sx_ss.at[d], sx_rs.at[d], {"token": to * 2 + core})

    def tz_copy(d):
        return z_copy(tz_send, tz_recv, tz_ss, tz_rs, d)

    def sz_copy(d):
        return z_copy(sz_send, sz_recv, sz_ss, sz_rs, d)

    def to_z(landed, send, recv, make, z_make):
        each(1, 4, make, arrive)
        total = jnp.sum(landed[...].astype(F32), axis=0).reshape(4, 64, 128)
        for half in range(2):
            mine = total[:, :, half * 64 : half * 64 + 64]
            send[half * 4 : half * 4 + 4] = jnp.concatenate([mine[:, :32], mine[:, 32:]], axis=2).astype(BF16)
        each(1, 8, z_make, start)
        recv[zslot] = send[zslot]

    def after_z(recv, out, make):
        each(1, 8, make, arrive)
        total = jnp.sum(recv[...].astype(F32), axis=0)
        out[...] = jnp.concatenate([total[:, :64], total[:, 64:]], axis=0)

    each(0, 4, tf_copy, arrive)
    each(1, 8, to_copy, arrive)
    rows_o = tattn_all[...].reshape(1024, 128)
    for block in range(4):
        rows_g = tg_all[:, :, block * 256 : block * 256 + 256].reshape(1024, 256)
        part = rows_dot(rows_o, rows_g).T.astype(BF16)
        for i in range(4):
            ty_send[i, block * 64 : block * 64 + 64, :] = part[i * 64 : i * 64 + 64]
    each(1, 4, ty_copy, start)
    ty_recv[y] = ty_send[y]

    sy_copies[1].wait_recv()
    sy_copies[2].wait_recv()
    total = spart[y].astype(F32) + sy_b[...].astype(F32) + sy_c[...].astype(F32)
    for i in range(4):
        sx_send[i] = total[:, i * 128 : i * 128 + 128].astype(BF16)
    each(1, 4, sx_copy, start)
    sx_recv[x] = sx_send[x]

    to_z(ty_recv, tz_send, tz_recv, ty_copy, tz_copy)
    to_z(sx_recv, sz_send, sz_recv, sx_copy, sz_copy)

    for chunk in range(CHUNKS):
        each(1, 16, lambda d: tb_copy(chunk, d), arrive)
        for a in range(3):
            block = tb_recv[chunk, :, a * 16 : a * 16 + 16, :].astype(F32).reshape(16, 2, 8, 256)
            for half in range(2):
                rows = rows_dot(shuffle, block[:, half].reshape(128, 256).astype(BF16)).astype(BF16)
                for i in range(2):
                    at = (2 * (2 * half + i) + chunk) * 128
                    tout[a, :, :, at : at + 128] = rows[:, i * 128 : i * 128 + 128].reshape(8, 16, 128)
    store = pltpu.make_async_copy(tout, tout_hbm, out_sem)
    store.start()

    after_z(sz_recv, sproj_out, sz_copy)
    after_z(tz_recv, tproj_out, tz_copy)

    each(1, 8, sb_copy, arrive)
    each(1, 16, tg_copy, leave)
    for chunk in range(CHUNKS):
        each(1, 16, lambda d: tc_copy(chunk, d), leave)
        each(1, 16, lambda d: tb_copy(chunk, d), leave)
    each(1, 8, sg_copy, leave)
    each(1, 8, sq_copy, leave)
    each(1, 8, sb_copy, leave)
    each(1, 4, sx_copy, leave)
    each(1, 4, ta_copy, leave)
    each(0, 4, tf_copy, leave)
    each(1, 8, to_copy, leave)
    each(1, 4, ty_copy, leave)
    each(1, 8, sz_copy, leave)
    each(1, 8, tz_copy, leave)
    for copy in [sg_pair, sattn_pair] + sy_copies:
        copy.wait_send()
    own_b.wait()
    store.wait()


def local(temporal_qkv, spatial_qkv, out_grad, temporal_proj, spatial_proj):
    def vm(*shape):
        return pltpu.VMEM(shape, BF16)

    def dma(*shape):
        return pltpu.SemaphoreType.DMA(shape)

    any_spec = pl.BlockSpec(memory_space=pl.ANY)
    vmem_spec = pl.BlockSpec(memory_space=pltpu.VMEM)
    tout, sout, tproj, sproj = pl.pallas_call(
        body,
        out_shape=(
            jax.ShapeDtypeStruct((3, 8, 16, 1024), BF16),
            jax.ShapeDtypeStruct((3, 8, 16, 1024), BF16),
            jax.ShapeDtypeStruct((64, 64), F32),
            jax.ShapeDtypeStruct((64, 64), F32),
        ),
        in_specs=[any_spec] * 5,
        out_specs=(any_spec, any_spec, vmem_spec, vmem_spec),
        scratch_shapes=[
            vm(3, 8, 16, 1024), vm(8, 16, 1024), vm(1024, 1024), vm(1024, 1024),
            vm(16, 16, 512), vm(16, 16, 512), vm(2, 16, 48, 256), vm(2, 16, 48, 256),
            vm(8, 128, 1024), vm(128, 1024), vm(3, 128, 512), pltpu.VMEM((3, 128, 512), F32),
            vm(2, 16, 48, 256), vm(2, 16, 48, 256), vm(3, 8, 16, 1024), vm(8, 128, 128),
            vm(128, 1024), vm(3, 128, 1024), vm(128, 1024), vm(3, 128, 1024), vm(2, 128, 512),
            vm(8, 128, 128), vm(128, 1024), vm(128, 512),
            vm(4, 256, 128), vm(4, 256, 128), vm(8, 32, 128), vm(8, 32, 128),
            vm(4, 256, 512), vm(256, 512), vm(256, 512), vm(256, 512), vm(256, 512),
            vm(4, 256, 128), vm(4, 256, 128), vm(8, 32, 128), vm(8, 32, 128),
            dma(4), dma(16), dma(16), dma(2, 16), dma(2, 16), dma(2, 16), dma(2, 16),
            dma(8), dma(8), dma(8), dma(8), dma(8), dma(8), dma(3),
            dma(2), dma(2), dma(4), dma(4), dma(4), dma(4), dma(8), dma(8), dma(3), dma(3), dma(4), dma(4), dma(4), dma(4),
            dma(8), dma(8), dma(8), dma(8), pltpu.SemaphoreType.DMA,
        ],
        compiler_params=pltpu.CompilerParams(
            collective_id=0, has_side_effects=True, vmem_limit_bytes=60 * 1024 * 1024
        ),
    )(
        temporal_qkv.reshape(3, 8, 16, 1024),
        spatial_qkv.reshape(3, 8, 16, 1024),
        out_grad.reshape(8, 16, 1024),
        temporal_proj,
        spatial_proj,
    )
    shape = (3, 1, 8, 16, 1024)
    return tout.reshape(shape), sout.reshape(shape), tproj, sproj


def solution(mesh):
    in_specs = (
        P(None, "dp", "frame", "token", None),
        P(None, "dp", "frame", "token", None),
        P("dp", "frame", "token", None),
        P(),
        P(),
    )
    out_specs = (
        P(None, "dp", "frame", "token", None),
        P(None, "dp", "frame", "token", None),
        P("frame", ("token", "dp")),
        P("frame", ("token", "dp")),
    )
    return jax.shard_map(local, mesh=mesh, in_specs=in_specs, out_specs=out_specs, check_vma=False)
```

```python
import jax
import jax.numpy as jnp
from jax import lax
from jax.experimental import pallas as pl
from jax.experimental.pallas import tpu as pltpu
from jax.sharding import PartitionSpec as P

MESH = pl.DeviceIdType.MESH
BF16 = jnp.bfloat16
F32 = jnp.float32
ROOT = 0.125
CHUNKS = 2
PAIRS = 4


def rows_dot(left, right):
    return lax.dot_general(left, right, (((0,), (0,)), ((), ())), preferred_element_type=F32)


def cols_dot(left, right):
    return lax.dot_general(left, right, (((1,), (1,)), ((), ())), preferred_element_type=F32)


def dot(left, right):
    return jnp.dot(left, right, preferred_element_type=F32)


def attend_pair(q, k, v, g):
    lane = lax.broadcasted_iota(jnp.int32, (128, 128), 1)
    low = lane < 64
    low_b = low.astype(F32).astype(BF16)
    high_b = (lane >= 64).astype(F32).astype(BF16)
    q2 = jnp.concatenate([q * low_b, q * high_b], axis=0)
    g2 = jnp.concatenate([g * low_b, g * high_b], axis=0)
    scores = cols_dot(q2, k)
    top = jnp.max(scores, axis=1, keepdims=True)
    grown = jnp.exp((scores - top) * ROOT)
    probs = grown * (1.0 / jnp.sum(grown, axis=1, keepdims=True))
    probs_low = probs.astype(BF16)
    out2 = dot(probs_low, v)
    out = jnp.where(low, out2[:128], out2[128:]).astype(BF16)
    prob_grad = cols_dot(g2, v)
    out_f = out.astype(F32)
    delta = jnp.sum(g2.astype(F32) * jnp.concatenate([out_f, out_f], axis=0), axis=1, keepdims=True)
    score_grad = (probs * (prob_grad - delta)).astype(BF16)
    dq2 = dot(score_grad, k)
    dq = jnp.where(low, dq2[:128], dq2[128:]) * ROOT
    dk = rows_dot(score_grad, q2) * ROOT
    dv = rows_dot(probs_low, g2)
    return out, dq, dk, dv


def shuffle_matrix():
    row = lax.broadcasted_iota(jnp.int32, (128, 128), 0)
    col = lax.broadcasted_iota(jnp.int32, (128, 128), 1)
    hit = ((row >> 3) == (col & 15)) & ((row & 7) == (col >> 4))
    return hit.astype(F32).astype(BF16)


def body(
    tqkv_hbm, squkv_hbm, grad_hbm, tproj_hbm, sproj_hbm,
    tout_hbm, sout_hbm, tproj_out, sproj_out,
    tqkv, grad, tproj, sproj,
    tg_send, tg_recv, tc_send, tc_recv, tg_all, tbranch, tchunk, tgrad, tb_send, tb_recv, tout, tattn,
    sg, sq, sbranch, sgrad, sattn,
    tattn_all, sg_peer, sattn_peer,
    ty_send, ty_recv, tz_send, tz_recv,
    spart, sy_a, sy_b, sy_c, sy_sum, sx_send, sx_recv, sz_send, sz_recv,
    load_sem, tg_ss, tg_rs, tc_ss, tc_rs, tb_ss, tb_rs,
    sg_ss, sg_rs, sq_ss, sq_rs, sb_ss, sb_rs, own_sem,
    pair_ss, pair_rs, ta_ss, ta_rs, tf_ss, tf_rs, to_ss, to_rs, ring_ss, ring_rs, ty_ss, ty_rs, sx_ss, sx_rs, tz_ss, tz_rs, sz_ss, sz_rs, out_sem,
):
    frame = lax.axis_index("frame")
    token = lax.axis_index("token")
    dp = lax.axis_index("dp")
    z, y = frame // 4, lax.rem(frame, 4)
    x, core = token // 2, lax.rem(token, 2)
    zslot = dp * 4 + z

    def frame_peer(d):
        return lax.rem(frame + d, 16)

    def token_peer(d):
        return lax.rem(token + d, 8)

    def x_peer(d):
        return lax.rem(x + d, 4) * 2 + core

    def y_peer(d):
        return z * 4 + lax.rem(y + d, 4)

    def remote(src, dst, send_sem, recv_sem, device):
        return pltpu.make_async_remote_copy(
            src_ref=src, dst_ref=dst, send_sem=send_sem, recv_sem=recv_sem, device_id=device, device_id_type=MESH
        )

    loads = [
        pltpu.make_async_copy(grad_hbm, grad, load_sem.at[0]),
        pltpu.make_async_copy(tqkv_hbm, tqkv, load_sem.at[1]),
        pltpu.make_async_copy(tproj_hbm, tproj, load_sem.at[2]),
        pltpu.make_async_copy(sproj_hbm, sproj, load_sem.at[3]),
    ]
    for load in loads:
        load.start()

    barrier = pltpu.get_barrier_semaphore()

    def greet_frame(d, carry):
        pl.semaphore_signal(barrier, inc=1, device_id={"frame": frame_peer(d)}, device_id_type=MESH)
        return carry

    def greet_token(d, carry):
        pl.semaphore_signal(barrier, inc=1, device_id={"token": token_peer(d)}, device_id_type=MESH)
        return carry

    def greet_dp(d, carry):
        pl.semaphore_signal(
            barrier, inc=1, device_id={"dp": 1 - dp, "frame": lax.rem(z + d, 4) * 4 + y}, device_id_type=MESH
        )
        return carry

    lax.fori_loop(1, 16, greet_frame, 0)
    lax.fori_loop(1, 8, greet_token, 0)
    lax.fori_loop(0, 4, greet_dp, 0)

    shuffle = shuffle_matrix()
    loads[0].wait()
    halves = []
    for half in range(2):
        rows = dot(shuffle, grad[:, :, half * 512 : half * 512 + 512].reshape(128, 512))
        halves.append(rows.reshape(16, 8, 512))
    tg_send[...] = jnp.concatenate(halves, axis=1).astype(BF16)

    loads[1].wait()
    for chunk in range(CHUNKS):
        for a in range(3):
            pieces = []
            for i in range(PAIRS):
                at = (2 * i + chunk) * 128
                rows = dot(shuffle, tqkv[a, :, :, at : at + 128].reshape(128, 128))
                pieces.append(rows.reshape(16, 8, 128))
            first = jnp.concatenate(pieces[:2], axis=2)
            second = jnp.concatenate(pieces[2:], axis=2)
            tc_send[chunk, :, a * 16 : a * 16 + 16, :] = jnp.concatenate([first, second], axis=1).astype(BF16)
        tc_recv[chunk, frame] = tc_send[chunk, frame]
    tg_recv[frame] = tg_send[frame]

    pl.semaphore_wait(barrier, 26)

    def tg_copy(d):
        peer = frame_peer(d)
        return remote(tg_send.at[peer], tg_recv.at[frame], tg_ss.at[d], tg_rs.at[d], {"frame": peer})

    def tc_copy(chunk, d):
        peer = frame_peer(d)
        return remote(
            tc_send.at[chunk, peer], tc_recv.at[chunk, frame], tc_ss.at[chunk, d], tc_rs.at[chunk, d], {"frame": peer}
        )

    def tb_copy(chunk, d):
        peer = frame_peer(d)
        return remote(
            tb_send.at[chunk, peer], tb_recv.at[chunk, frame], tb_ss.at[chunk, d], tb_rs.at[chunk, d], {"frame": peer}
        )

    def token_rows(who):
        return pl.ds(pl.multiple_of(who * 16, 16), 16)

    def sg_copy(d):
        peer = token_peer(d)
        return remote(grad_hbm.at[peer], sg.at[token_rows(token)], sg_ss.at[d], sg_rs.at[d], {"token": peer})

    def sq_copy(d):
        peer = token_peer(d)
        return remote(squkv_hbm.at[:, peer], sq.at[:, token_rows(token)], sq_ss.at[d], sq_rs.at[d], {"token": peer})

    def sb_copy(d):
        peer = token_peer(d)
        return remote(sgrad.at[:, token_rows(peer)], sout_hbm.at[:, token], sb_ss.at[d], sb_rs.at[d], {"token": peer})

    def each(low, high, make, act):
        def step(d, carry):
            act(make(d))
            return carry

        lax.fori_loop(low, high, step, 0)

    def start(copy):
        copy.start()

    def arrive(copy):
        copy.wait_recv()

    def leave(copy):
        copy.wait_send()

    each(1, 16, tg_copy, start)
    each(1, 8, sg_copy, start)
    own_g = pltpu.make_async_copy(grad_hbm.at[token], sg.at[token_rows(token)], own_sem.at[0])
    own_q = pltpu.make_async_copy(squkv_hbm.at[:, token], sq.at[:, token_rows(token)], own_sem.at[1])
    own_g.start()
    own_q.start()
    each(1, 8, sq_copy, start)

    each(1, 16, lambda d: tc_copy(0, d), start)
    each(1, 16, lambda d: tc_copy(1, d), start)

    peer_core = {"token": token + 1 - 2 * core}
    each(1, 16, tg_copy, arrive)
    loads[2].wait()
    landed = tg_recv[...].astype(F32).reshape(16, 2, 8, 512)
    for half in range(2):
        tg_all[token, :, half * 512 : half * 512 + 512] = landed[:, half].reshape(128, 512).astype(BF16)

    def ta_copy(d):
        to = lax.rem(x + d, 4) * 2 + core
        return remote(tg_all.at[token], tg_all.at[token], ta_ss.at[d], ta_rs.at[d], {"token": to})

    def tf_copy(d):
        of = lax.rem(x + 4 - d, 4) * 2 + core
        return remote(tg_all.at[of], tg_all.at[of], tf_ss.at[d], tf_rs.at[d], peer_core)

    each(1, 4, ta_copy, start)
    tf_copy(0).start()
    for col in range(0, 1024, 256):
        tbranch[:, col : col + 256] = dot(tg_all[token], tproj[:, col : col + 256]).astype(BF16)

    own_g.wait()
    each(1, 8, sg_copy, arrive)
    loads[3].wait()
    sg_pair = remote(sg, sg_peer, pair_ss.at[0], pair_rs.at[0], peer_core)
    sg_pair.start()
    for col in range(0, 1024, 256):
        sbranch[:, col : col + 256] = dot(sg[...], sproj[:, col : col + 256]).astype(BF16)

    def to_copy(d):
        peer = token_peer(d)
        return remote(tattn.at[peer], tattn_all.at[token], to_ss.at[d], to_rs.at[d], {"token": peer})

    def temporal_chunk(chunk):
        each(1, 16, lambda d: tc_copy(chunk, d), arrive)
        for a in range(3):
            block = tc_recv[chunk, :, a * 16 : a * 16 + 16, :].astype(F32).reshape(16, 2, 8, 256)
            for half in range(2):
                tchunk[a, :, half * 256 : half * 256 + 256] = block[:, half].reshape(128, 256).astype(BF16)

        def pair(i, carry):
            here = pl.ds(pl.multiple_of(i * 128, 128), 128)
            there = pl.ds(pl.multiple_of((2 * i + chunk) * 128, 128), 128)
            out, dq, dk, dv = attend_pair(tchunk[0, :, here], tchunk[1, :, here], tchunk[2, :, here], tbranch[:, there])
            tattn[2 * i + chunk] = out
            tgrad[0, :, here] = dq
            tgrad[1, :, here] = dk
            tgrad[2, :, here] = dv
            return carry

        lax.fori_loop(0, PAIRS, pair, 0, unroll=True)
        if chunk == 1:
            each(1, 8, to_copy, start)
            tattn_all[token] = tattn[token]
        for a in range(3):
            rows = tgrad[a].reshape(16, 8, 512)
            tb_send[chunk, :, a * 16 : a * 16 + 16, :] = jnp.concatenate(
                [rows[:, :, :256], rows[:, :, 256:]], axis=1
            ).astype(BF16)
        each(1, 16, lambda d: tb_copy(chunk, d), start)
        tb_recv[chunk, frame] = tb_send[chunk, frame]

    sattn_pair = remote(sattn.at[1 - core], sattn_peer, pair_ss.at[1], pair_rs.at[1], peer_core)
    left, right = 3 - 2 * core, 1 + 2 * core
    left_y, right_y = {"frame": y_peer(left)}, {"frame": y_peer(right)}
    sy_copies = [
        remote(spart.at[lax.rem(y + 2, 4)], sy_a, ring_ss.at[0], ring_rs.at[0], left_y),
        remote(spart.at[lax.rem(y + right, 4)], sy_b, ring_ss.at[1], ring_rs.at[1], right_y),
        remote(sy_sum, sy_c, ring_ss.at[2], ring_rs.at[2], left_y),
    ]

    temporal_chunk(0)

    own_q.wait()
    each(1, 8, sq_copy, arrive)

    def spatial_pair(i, carry):
        for c in range(2):
            at = pl.ds(pl.multiple_of((2 * i + c) * 128, 128), 128)
            here = pl.ds(pl.multiple_of(i * 128, 128), 128)
            out, dq, dk, dv = attend_pair(sq[0, :, at], sq[1, :, at], sq[2, :, at], sbranch[:, at])
            sattn[c, :, here] = out
            sgrad[0, :, at] = dq.astype(BF16)
            sgrad[1, :, at] = dk.astype(BF16)
            sgrad[2, :, at] = dv.astype(BF16)
        return carry

    lax.fori_loop(0, 4, spatial_pair, 0, unroll=True)
    sattn_pair.start()
    each(1, 8, sb_copy, start)
    own_b = pltpu.make_async_copy(sgrad.at[:, token_rows(token)], sout_hbm.at[:, token], own_sem.at[2])
    own_b.start()

    sg_pair.wait_recv()
    sattn_pair.wait_recv()
    rows_g = jnp.concatenate([sg[...], sg_peer[...]], axis=0)
    rows_o = jnp.concatenate([sattn[core], sattn_peer[...]], axis=0)
    for block in range(4):
        part = rows_dot(rows_g[:, block * 256 : block * 256 + 256], rows_o).astype(BF16)
        for i in range(4):
            spart[i, block * 64 : block * 64 + 64, :] = part[i * 64 : i * 64 + 64]
    sy_copies[0].start()
    sy_copies[1].start()

    each(1, 4, ta_copy, arrive)
    each(1, 4, tf_copy, start)

    temporal_chunk(1)

    sy_copies[0].wait_recv()
    sy_sum[...] = (spart[lax.rem(y + left, 4)].astype(F32) + sy_a[...].astype(F32)).astype(BF16)
    sy_copies[2].start()


    def z_copy(send, recv, ss, rs, d):
        to = lax.rem(zslot + d, 8)
        return remote(send.at[to], recv.at[zslot], ss.at[d], rs.at[d], {"dp": to // 4, "frame": lax.rem(to, 4) * 4 + y})

    def ty_copy(d):
        to = lax.rem(y + d, 4)
        return remote(ty_send.at[to], ty_recv.at[y], ty_ss.at[d], ty_rs.at[d], {"frame": z * 4 + to})

    def sx_copy(d):
        to = lax.rem(x + d, 4)
        return remote(sx_send.at[to], sx_recv.at[x], sx_ss.at[d], sx_rs.at[d], {"token": to * 2 + core})

    def tz_copy(d):
        return z_copy(tz_send, tz_recv, tz_ss, tz_rs, d)

    def sz_copy(d):
        return z_copy(sz_send, sz_recv, sz_ss, sz_rs, d)

    def to_z(landed, send, recv, make, z_make):
        each(1, 4, make, arrive)
        total = jnp.sum(landed[...].astype(F32), axis=0).reshape(4, 64, 128)
        for half in range(2):
            mine = total[:, :, half * 64 : half * 64 + 64]
            send[half * 4 : half * 4 + 4] = jnp.concatenate([mine[:, :32], mine[:, 32:]], axis=2).astype(BF16)
        each(1, 8, z_make, start)
        recv[zslot] = send[zslot]

    def after_z(recv, out, make):
        each(1, 8, make, arrive)
        total = jnp.sum(recv[...].astype(F32), axis=0)
        out[...] = jnp.concatenate([total[:, :64], total[:, 64:]], axis=0)

    each(0, 4, tf_copy, arrive)
    each(1, 8, to_copy, arrive)
    rows_o = tattn_all[...].reshape(1024, 128)
    for block in range(4):
        rows_g = tg_all[:, :, block * 256 : block * 256 + 256].reshape(1024, 256)
        part = rows_dot(rows_o, rows_g).T.astype(BF16)
        for i in range(4):
            ty_send[i, block * 64 : block * 64 + 64, :] = part[i * 64 : i * 64 + 64]
    each(1, 4, ty_copy, start)
    ty_recv[y] = ty_send[y]

    sy_copies[1].wait_recv()
    sy_copies[2].wait_recv()
    total = spart[y].astype(F32) + sy_b[...].astype(F32) + sy_c[...].astype(F32)
    for i in range(4):
        sx_send[i] = total[:, i * 128 : i * 128 + 128].astype(BF16)
    each(1, 4, sx_copy, start)
    sx_recv[x] = sx_send[x]

    to_z(ty_recv, tz_send, tz_recv, ty_copy, tz_copy)
    to_z(sx_recv, sz_send, sz_recv, sx_copy, sz_copy)

    for chunk in range(CHUNKS):
        each(1, 16, lambda d: tb_copy(chunk, d), arrive)
        for a in range(3):
            block = tb_recv[chunk, :, a * 16 : a * 16 + 16, :].astype(F32).reshape(16, 2, 8, 256)
            for half in range(2):
                rows = rows_dot(shuffle, block[:, half].reshape(128, 256).astype(BF16)).astype(BF16)
                for i in range(2):
                    at = (2 * (2 * half + i) + chunk) * 128
                    tout[a, :, :, at : at + 128] = rows[:, i * 128 : i * 128 + 128].reshape(8, 16, 128)
    store = pltpu.make_async_copy(tout, tout_hbm, out_sem)
    store.start()

    after_z(sz_recv, sproj_out, sz_copy)
    after_z(tz_recv, tproj_out, tz_copy)

    each(1, 8, sb_copy, arrive)
    each(1, 16, tg_copy, leave)
    for chunk in range(CHUNKS):
        each(1, 16, lambda d: tc_copy(chunk, d), leave)
        each(1, 16, lambda d: tb_copy(chunk, d), leave)
    each(1, 8, sg_copy, leave)
    each(1, 8, sq_copy, leave)
    each(1, 8, sb_copy, leave)
    each(1, 4, sx_copy, leave)
    each(1, 4, ta_copy, leave)
    each(0, 4, tf_copy, leave)
    each(1, 8, to_copy, leave)
    each(1, 4, ty_copy, leave)
    each(1, 8, sz_copy, leave)
    each(1, 8, tz_copy, leave)
    for copy in [sg_pair, sattn_pair] + sy_copies:
        copy.wait_send()
    own_b.wait()
    store.wait()


def local(temporal_qkv, spatial_qkv, out_grad, temporal_proj, spatial_proj):
    def vm(*shape):
        return pltpu.VMEM(shape, BF16)

    def dma(*shape):
        return pltpu.SemaphoreType.DMA(shape)

    any_spec = pl.BlockSpec(memory_space=pl.ANY)
    vmem_spec = pl.BlockSpec(memory_space=pltpu.VMEM)
    tout, sout, tproj, sproj = pl.pallas_call(
        body,
        out_shape=(
            jax.ShapeDtypeStruct((3, 8, 16, 1024), BF16),
            jax.ShapeDtypeStruct((3, 8, 16, 1024), BF16),
            jax.ShapeDtypeStruct((64, 64), F32),
            jax.ShapeDtypeStruct((64, 64), F32),
        ),
        in_specs=[any_spec] * 5,
        out_specs=(any_spec, any_spec, vmem_spec, vmem_spec),
        scratch_shapes=[
            vm(3, 8, 16, 1024), vm(8, 16, 1024), vm(1024, 1024), vm(1024, 1024),
            vm(16, 16, 512), vm(16, 16, 512), vm(2, 16, 48, 256), vm(2, 16, 48, 256),
            vm(8, 128, 1024), vm(128, 1024), vm(3, 128, 512), pltpu.VMEM((3, 128, 512), F32),
            vm(2, 16, 48, 256), vm(2, 16, 48, 256), vm(3, 8, 16, 1024), vm(8, 128, 128),
            vm(128, 1024), vm(3, 128, 1024), vm(128, 1024), vm(3, 128, 1024), vm(2, 128, 512),
            vm(8, 128, 128), vm(128, 1024), vm(128, 512),
            vm(4, 256, 128), vm(4, 256, 128), vm(8, 32, 128), vm(8, 32, 128),
            vm(4, 256, 512), vm(256, 512), vm(256, 512), vm(256, 512), vm(256, 512),
            vm(4, 256, 128), vm(4, 256, 128), vm(8, 32, 128), vm(8, 32, 128),
            dma(4), dma(16), dma(16), dma(2, 16), dma(2, 16), dma(2, 16), dma(2, 16),
            dma(8), dma(8), dma(8), dma(8), dma(8), dma(8), dma(3),
            dma(2), dma(2), dma(4), dma(4), dma(4), dma(4), dma(8), dma(8), dma(3), dma(3), dma(4), dma(4), dma(4), dma(4),
            dma(8), dma(8), dma(8), dma(8), pltpu.SemaphoreType.DMA,
        ],
        compiler_params=pltpu.CompilerParams(
            collective_id=0, has_side_effects=True, vmem_limit_bytes=60 * 1024 * 1024
        ),
    )(
        temporal_qkv.reshape(3, 8, 16, 1024),
        spatial_qkv.reshape(3, 8, 16, 1024),
        out_grad.reshape(8, 16, 1024),
        temporal_proj,
        spatial_proj,
    )
    shape = (3, 1, 8, 16, 1024)
    return tout.reshape(shape), sout.reshape(shape), tproj, sproj


def solution(mesh):
    in_specs = (
        P(None, "dp", "frame", "token", None),
        P(None, "dp", "frame", "token", None),
        P("dp", "frame", "token", None),
        P(),
        P(),
    )
    out_specs = (
        P(None, "dp", "frame", "token", None),
        P(None, "dp", "frame", "token", None),
        P("frame", ("token", "dp")),
        P("frame", ("token", "dp")),
    )
    return jax.shard_map(local, mesh=mesh, in_specs=in_specs, out_specs=out_specs, check_vma=False)
```
